32 devices in a mesh: blk: 8 (over y, x, core), path: 4 (over z).
Axes of the slice: x: 2, y: 2, z: 4, core: 2. Of those that a mesh axis runs over, the one named last changes fastest.
Arguments:
- records: bfloat16 [8192, 512], P('blk'), may hold values from -87.98545 to 87.98545
- coefficients: float32 [8192, 64], P('blk', 'path'), may hold values from -6 to 6
- velocity: float32 [8192, 64], P('blk', 'path'), may hold values from -3 to 3
- targets: float32 [8192, 64], P('blk', 'path'), may hold values from -6 to 6
- block_local: int32 [3, 192], P(None, 'blk'), may hold values from 0 to 1023
- block_count: int32 [3, 8], replicated, may hold values from 1 to 24, 128 in all within a row
- candidates: bfloat16 [4096, 512], P('blk'), may hold values from -87.98545 to 87.98545
- frequencies: bfloat16 [512, 1024], replicated, may hold values from -0.25 to 0.25
- phases: float32 [1024], replicated, may hold values from -3.140625 to 3.140625
- prior_weight: float32 [1024, 64], P(None, 'path'), may hold values from -6 to 6
Outputs:
- coefficients_out: float32 [8192, 64], P('blk', 'path')
- velocity_out: float32 [8192, 64], P('blk', 'path')
- scores: float32 [4096, 64], P('blk', 'path')
- path_rms: float32 [4096], P('blk')
The draws below stay inside these ranges and needn't reach their ends.
Inputs may be any that keep to these rules, and one draw needn't show every extreme that they name: `block_count`: each row sums to 128, and its largest entry is exactly 24. `block_local`: index within the owner's records; a slot at or beyond the owner's count in that step is not used. Used entries of one owner may repeat.
All inputs are finite; a program needn't handle non-finite values.
Results may differ from the reference program's by a relative error of at most 0.0014.
Values may be sent and summed in bfloat16 or wider, within the bound.
A program may use at most 128 MiB of HBM per device.

```python
import math
import jax
import jax.numpy as jnp
import numpy as np
from jax import lax

D = 512
FEATS = 1024
PATHS = 64
STEPS = 3
REC_DEV = 1024
CAND_DEV = 512
CAP = 24
BLOCK = 128
RECORDS = 8192
CANDIDATES = 4096
N_BLK = 8


def column_spread(key, power, level):
    order = jax.random.permutation(jax.random.fold_in(key, 4099), D)
    rank = order.astype(jnp.float32)
    return jnp.sqrt(level * D * (rank + 1.0) ** (-power))


def draw_records(key, part):
    spread = column_spread(key, 1.5, 0.42)
    noise = jax.random.truncated_normal(jax.random.fold_in(key, 11), -6.0, 6.0, (RECORDS, D), jnp.float32)
    return (noise * spread[None, :]).astype(jnp.bfloat16)


def draw_candidates(key, part):
    spread = column_spread(key, 1.5, 0.42)
    noise = jax.random.truncated_normal(jax.random.fold_in(key, 12), -6.0, 6.0, (CANDIDATES, D), jnp.float32)
    return (noise * spread[None, :]).astype(jnp.bfloat16)


def plant(values, stream_key, low, top_value):
    place = [jax.random.randint(jax.random.fold_in(stream_key, axis), (), 0, length) for axis, length in enumerate(values.shape)]
    main_axis = values.shape.index(max(values.shape))
    beside = place[:main_axis] + [(place[main_axis] + 1) % values.shape[main_axis]] + place[main_axis + 1:]
    return values.at[tuple(place)].set(low).at[tuple(beside)].set(top_value)


def levels(own_key, extent, pieces, least, top_value):
    loudness, own = 1.0, jax.random.fold_in(own_key, 6)
    for position, parts in pieces:
        steps = jnp.exp(jax.random.uniform(jax.random.fold_in(own, position), (parts,), jnp.float32, least / len(pieces), top_value / len(pieces)))
        loudness = loudness * jnp.repeat(steps, extent[position] // parts).reshape([-1 if axis == position else 1 for axis in range(len(extent))])
    return loudness


def profile(count, total, most, skew):
    loads = [(1 << 20) // math.isqrt(grade ** skew) + 1 for grade in range(2, count + 1)]
    spare, counts = total - most - (count - 1), [1] * (count - 1)
    while spare > 0:
        free = [i for i in range(count - 1) if counts[i] < most]
        pool, left = sum([loads[i] for i in free]), spare
        for i in free:
            extra = min(most - counts[i], max(1, left * loads[i] // pool), spare)
            counts[i] = counts[i] + extra
            spare = spare - extra
    return np.array([most] + counts)


def uneven(key, amount, total, most, slope):
    if amount == 2:
        one = jax.random.randint(key, (), max(1, total - most), min(most, total - 1) + 1)
        return jnp.stack([one, total - one])
    lengths = jnp.asarray(profile(amount, total, most, slope), jnp.int32)
    twos = (amount - 1) // 2
    source_of, sink = lengths[1:1 + 2 * twos:2], lengths[2:2 + 2 * twos:2]
    slack = jnp.minimum(source_of - 1, most - sink)
    moved = jax.random.randint(jax.random.fold_in(key, 1), (twos,), 0, 1 << 20) % (slack + 1)
    lengths = lengths.at[1:1 + 2 * twos:2].set(source_of - moved).at[2:2 + 2 * twos:2].set(sink + moved)
    return lengths[jax.random.permutation(jax.random.fold_in(key, 2), amount)]


def centred(own_key, shape, deviation, limit, split=(), held_as=jnp.bfloat16):
    gain = levels(own_key, shape, split, -0.22, 0.18) if split else 1.0
    values = jax.random.normal(own_key, shape, jnp.float32) * deviation * gain
    return jnp.minimum(jnp.maximum(values, -limit), limit).astype(held_as)


def setup_inputs(seed: int = 0) -> dict:
    arg_keys = jax.random.split(jax.random.key(seed), 11)
    records = draw_records(jax.random.fold_in(arg_keys[10], 71), 0)
    coefficients = centred(arg_keys[1], (RECORDS, PATHS), 1.0, 6.0, ((0, 8), (1, 4)), jnp.float32)
    velocity = centred(arg_keys[2], (RECORDS, PATHS), 0.2, 3.0, ((0, 8), (1, 4)), jnp.float32)
    targets = centred(arg_keys[3], (RECORDS, PATHS), 1.0, 6.0, ((0, 8), (1, 4)), jnp.float32)
    block_local = plant(jax.random.randint(arg_keys[4], (STEPS, N_BLK * CAP), 0, REC_DEV), jax.random.fold_in(arg_keys[4], 1), 0, REC_DEV - 1).astype(jnp.int32)
    block_count = jax.vmap(lambda own: uneven(own, N_BLK, BLOCK, CAP, 2))(jax.random.split(arg_keys[5], STEPS)).reshape((STEPS, N_BLK)).astype(jnp.int32)
    candidates = draw_candidates(jax.random.fold_in(arg_keys[10], 71), 0)
    frequencies = centred(arg_keys[7], (D, FEATS), D ** -0.5, 0.25)
    phases = jnp.clip(jax.random.uniform(arg_keys[8], (FEATS,), jnp.float32, -3.140625, 3.140625), -3.140625, 3.140625)
    prior_weight = centred(arg_keys[9], (FEATS, PATHS), 1.0, 6.0, ((1, 4),), jnp.float32)
    return dict(records=records, coefficients=coefficients, velocity=velocity, targets=targets, block_local=block_local, block_count=block_count, candidates=candidates, frequencies=frequencies, phases=phases, prior_weight=prior_weight)


NOISE = 0.5
MOMENTUM = 0.9
RATE = 0.3
EPSILON = 1e-06
SIGNAL = 9.0

def square_norms(row_block):
    widened = row_block.astype(jnp.float32)
    return lax.optimization_barrier(jnp.sum(widened * widened, axis=1))

def kernel_apply(left_rows, left_norms, right_rows, right_norms, weights):
    dot_values = lax.dot_general(left_rows, right_rows, (((1,), (1,)), ((), ())), preferred_element_type=jnp.float32)
    distance = left_norms[:, None] + right_norms[None, :] - 2.0 * dot_values
    kernel_tile = SIGNAL * jnp.exp(-distance / left_rows.shape[1])
    return jnp.dot(kernel_tile, weights, precision=lax.Precision.HIGHEST)

def prior_values(cand_rows, frequencies, phases, prior_weight):
    angles = jnp.dot(cand_rows, frequencies, preferred_element_type=jnp.float32) * math.sqrt(2.0) + phases[None, :]
    features = math.sqrt(2.0 * SIGNAL / frequencies.shape[1]) * jnp.cos(angles)
    return jnp.dot(features, prior_weight, precision=lax.Precision.HIGHEST)

def all_shards(left_rows, shard_rows, shard_norms, shard_coefs):
    left_norms = square_norms(left_rows)

    def accumulate(running, members):
        return (running + kernel_apply(left_rows, left_norms, members[0], members[1], members[2]), None)
    summed, _ = lax.scan(accumulate, jnp.zeros((left_rows.shape[0], PATHS), jnp.float32), (shard_rows, shard_norms, shard_coefs))
    return summed

def reference(records, coefficients, velocity, targets, block_local, block_count, candidates, frequencies, phases, prior_weight):
    root_count = jnp.sqrt(jnp.float32(RECORDS))
    record_norms = square_norms(records)
    shard_rows = records.reshape(N_BLK, REC_DEV, D)
    shard_norms = record_norms.reshape(N_BLK, REC_DEV)
    owners = jnp.arange(N_BLK, dtype=jnp.int32)[:, None]
    slot_ids = jnp.arange(CAP, dtype=jnp.int32)[None, :]
    for repeat in range(STEPS):
        local_rows = block_local[repeat].reshape(N_BLK, CAP)
        row_index = (owners * REC_DEV + local_rows).reshape(-1).astype(jnp.int32)
        is_live = (slot_ids < block_count[repeat][:, None]).reshape(-1)
        shard_coefs = coefficients.reshape(N_BLK, REC_DEV, PATHS)
        product = all_shards(records[row_index], shard_rows, shard_norms, shard_coefs) / root_count
        gradient = jnp.where(is_live[:, None], product + NOISE * coefficients[row_index] - targets[row_index], 0.0)
        velocity = (MOMENTUM * velocity).at[row_index].add(-RATE * gradient)
        coefficients = coefficients + velocity
    group_rows = candidates.reshape(N_BLK, CAND_DEV, D)
    shard_coefs = coefficients.reshape(N_BLK, REC_DEV, PATHS)

    def group_score(members):
        cand_group, first_rows, first_norms, first_coefs, second_rows, second_norms, second_coefs = members
        group_norms = square_norms(cand_group)
        first_part = prior_values(cand_group, frequencies, phases, prior_weight) + kernel_apply(cand_group, group_norms, first_rows, first_norms, first_coefs) / root_count
        return first_part + kernel_apply(cand_group, group_norms, second_rows, second_norms, second_coefs) / root_count

    def rolled(array_in):
        return jnp.roll(array_in, -1, axis=0)
    per_group = lax.map(group_score, (group_rows, shard_rows, shard_norms, shard_coefs, rolled(shard_rows), rolled(shard_norms), rolled(shard_coefs)))
    scores = jnp.roll(per_group, 2, axis=0).reshape(CANDIDATES, PATHS)
    path_rms = jnp.sqrt(lax.optimization_barrier(jnp.sum(scores * scores, axis=1)) / PATHS + EPSILON)
    return (coefficients, velocity, scores, path_rms)
```

```python
import math

import jax
import jax.numpy as jnp
from jax import lax
from jax.sharding import PartitionSpec as P

NOISE = 0.5
MOMENTUM = 0.9
RATE = 0.3
EPSILON = 1e-06
SIGNAL = 9.0


def passed_along(shard, axis, by):
    length = lax.axis_size(axis)
    return lax.ppermute(shard, axis, [(i, (i + by) % length) for i in range(length)])


def square_norms(row_block):
    widened = row_block.astype(jnp.float32)
    return jnp.sum(widened * widened, axis=-1)


def kernel_tile(left_rows, right_rows):
    dot_values = lax.dot_general(
        left_rows, right_rows, (((1,), (1,)), ((), ())), preferred_element_type=jnp.float32
    )
    distance = square_norms(left_rows)[:, None] + square_norms(right_rows)[None, :] - 2.0 * dot_values
    return SIGNAL * jnp.exp(-distance / left_rows.shape[1])


def product(left, right):
    return jnp.dot(left, right, precision=lax.Precision.HIGHEST)


def prior_values(cand_rows, frequencies, phases, prior_weight):
    angles = (
        jnp.dot(cand_rows, frequencies, preferred_element_type=jnp.float32) * math.sqrt(2.0)
        + phases[None, :]
    )
    features = math.sqrt(2.0 * SIGNAL / frequencies.shape[1]) * jnp.cos(angles)
    return product(features, prior_weight)


def geometric(first, last):
    return sum(MOMENTUM**i for i in range(first, last + 1))


def shards(
    records,
    coefficients,
    velocity,
    targets,
    block_local,
    block_count,
    candidates,
    frequencies,
    phases,
    prior_weight,
):
    n_blk = lax.axis_size("blk")
    record_total = records.shape[0] * n_blk
    root_count = jnp.sqrt(jnp.float32(record_total))
    steps, cap = block_local.shape
    own = lax.axis_index("blk")
    neighbour = passed_along(candidates, "blk", 1)
    picked = block_local.reshape(-1)
    gathered = lax.all_gather(records[picked], "blk", axis=0)
    ids = lax.all_gather(picked, "blk", axis=0) + (
        jnp.arange(n_blk, dtype=jnp.int32) * records.shape[0]
    )[:, None]
    rows, keys, partial = [], [], []
    for t in range(steps):
        part = slice(t * cap, (t + 1) * cap)
        rows.append(gathered[:, part].reshape(n_blk * cap, -1))
        keys.append(ids[:, part].reshape(-1))
        held = coefficients + geometric(1, t) * velocity
        local = product(kernel_tile(rows[t], records), held) / root_count
        mine = NOISE * held[block_local[t]] - targets[block_local[t]]
        before = lax.dynamic_slice_in_dim(local, own * cap, cap, 0)
        partial.append(lax.dynamic_update_slice_in_dim(local, before + mine, own * cap, 0))
    whole = lax.psum(jnp.stack(partial), "blk")
    moves = []
    for t in range(steps):
        gradient = whole[t]
        for s in range(t):
            link = kernel_tile(rows[t], rows[s]) / root_count + NOISE * (
                keys[t][:, None] == keys[s][None, :]
            ).astype(jnp.float32)
            gradient = gradient + geometric(0, t - 1 - s) * product(link, moves[s])
        live = (jnp.arange(cap, dtype=jnp.int32)[None, :] < block_count[t][:, None]).reshape(-1)
        moves.append(jnp.where(live[:, None], -RATE * gradient, 0.0))
    mine = [lax.dynamic_slice_in_dim(m, own * cap, cap, 0) for m in moves]
    speed = jnp.concatenate([MOMENTUM ** (steps - 1 - s) * m for s, m in enumerate(mine)])
    shift = jnp.concatenate([geometric(0, steps - 1 - s) * m for s, m in enumerate(mine)])
    both = jnp.concatenate(
        [
            coefficients + geometric(1, steps) * velocity,
            MOMENTUM**steps * velocity,
        ],
        axis=1,
    )
    both = both.at[picked].add(jnp.concatenate([shift, speed], axis=1))
    width = coefficients.shape[1]
    coefficients, velocity = both[:, :width], both[:, width:]
    own_sum = product(kernel_tile(candidates, records), coefficients)
    next_sum = product(kernel_tile(neighbour, records), coefficients)
    first_part = prior_values(candidates, frequencies, phases, prior_weight) + own_sum / root_count
    scores = passed_along(first_part, "blk", 2) + passed_along(next_sum / root_count, "blk", 1)
    squares_local = jnp.sum(scores * scores, axis=1)
    summed = lax.psum(squares_local, "path")
    path_rms = jnp.sqrt(summed / (scores.shape[1] * lax.axis_size("path")) + EPSILON)
    return (coefficients, velocity, scores, path_rms)


def solution(mesh):
    return jax.shard_map(
        shards,
        mesh=mesh,
        in_specs=(
            P("blk", None),
            P("blk", "path"),
            P("blk", "path"),
            P("blk", "path"),
            P(None, "blk"),
            P(),
            P("blk", None),
            P(),
            P(),
            P(None, "path"),
        ),
        out_specs=(P("blk", "path"), P("blk", "path"), P("blk", "path"), P("blk")),
        check_vma=False,
    )
```

```python
import functools
import math

import jax
import jax.numpy as jnp
from jax import lax
from jax.experimental import pallas as pl
from jax.experimental.pallas import tpu as pltpu
from jax.sharding import PartitionSpec as P

NOISE = 0.5
MOMENTUM = 0.9
RATE = 0.3
EPSILON = 1e-06
SIGNAL = 9.0


def passed_along(shard, axis, by):
    length = lax.axis_size(axis)
    return lax.ppermute(shard, axis, [(i, (i + by) % length) for i in range(length)])


def square_norms(row_block):
    widened = row_block.astype(jnp.float32)
    return jnp.sum(widened * widened, axis=-1)


def kernel_tile(left_rows, right_rows):
    dot_values = lax.dot_general(
        left_rows, right_rows, (((1,), (1,)), ((), ())), preferred_element_type=jnp.float32
    )
    distance = square_norms(left_rows)[:, None] + square_norms(right_rows)[None, :] - 2.0 * dot_values
    return SIGNAL * jnp.exp(-distance / left_rows.shape[1])


def product(left, right):
    return jnp.dot(left, right, precision=lax.Precision.HIGHEST)


def prior_values(cand_rows, frequencies, phases, prior_weight):
    angles = (
        jnp.dot(cand_rows, frequencies, preferred_element_type=jnp.float32) * math.sqrt(2.0)
        + phases[None, :]
    )
    features = math.sqrt(2.0 * SIGNAL / frequencies.shape[1]) * jnp.cos(angles)
    return product(features, prior_weight)


def geometric(first, last):
    return sum(MOMENTUM**i for i in range(first, last + 1))


def shards(
    records,
    coefficients,
    velocity,
    targets,
    block_local,
    block_count,
    candidates,
    frequencies,
    phases,
    prior_weight,
):
    n_blk = lax.axis_size("blk")
    record_total = records.shape[0] * n_blk
    root_count = jnp.sqrt(jnp.float32(record_total))
    steps, cap = block_local.shape
    own = lax.axis_index("blk")
    neighbour = passed_along(candidates, "blk", 1)
    picked = block_local.reshape(-1)
    gathered = lax.all_gather(records[picked], "blk", axis=0)
    ids = lax.all_gather(picked, "blk", axis=0) + (
        jnp.arange(n_blk, dtype=jnp.int32) * records.shape[0]
    )[:, None]
    rows, keys, partial = [], [], []
    for t in range(steps):
        part = slice(t * cap, (t + 1) * cap)
        rows.append(gathered[:, part].reshape(n_blk * cap, -1))
        keys.append(ids[:, part].reshape(-1))
        held = coefficients + geometric(1, t) * velocity
        local = product(kernel_tile(rows[t], records), held) / root_count
        mine = NOISE * held[block_local[t]] - targets[block_local[t]]
        before = lax.dynamic_slice_in_dim(local, own * cap, cap, 0)
        partial.append(lax.dynamic_update_slice_in_dim(local, before + mine, own * cap, 0))
    whole = lax.psum(jnp.stack(partial), "blk")
    moves = []
    for t in range(steps):
        gradient = whole[t]
        for s in range(t):
            link = kernel_tile(rows[t], rows[s]) / root_count + NOISE * (
                keys[t][:, None] == keys[s][None, :]
            ).astype(jnp.float32)
            gradient = gradient + geometric(0, t - 1 - s) * product(link, moves[s])
        live = (jnp.arange(cap, dtype=jnp.int32)[None, :] < block_count[t][:, None]).reshape(-1)
        moves.append(jnp.where(live[:, None], -RATE * gradient, 0.0))
    mine = [lax.dynamic_slice_in_dim(m, own * cap, cap, 0) for m in moves]
    speed = jnp.concatenate([MOMENTUM ** (steps - 1 - s) * m for s, m in enumerate(mine)])
    shift = jnp.concatenate([geometric(0, steps - 1 - s) * m for s, m in enumerate(mine)])
    both = jnp.concatenate(
        [
            coefficients + geometric(1, steps) * velocity,
            MOMENTUM**steps * velocity,
        ],
        axis=1,
    )
    both = both.at[picked].add(jnp.concatenate([shift, speed], axis=1))
    width = coefficients.shape[1]
    coefficients, velocity = both[:, :width], both[:, width:]
    own_sum = product(kernel_tile(candidates, records), coefficients)
    next_sum = product(kernel_tile(neighbour, records), coefficients)
    first_part = prior_values(candidates, frequencies, phases, prior_weight) + own_sum / root_count
    scores = passed_along(first_part, "blk", 2) + passed_along(next_sum / root_count, "blk", 1)
    squares_local = jnp.sum(scores * scores, axis=1)
    summed = lax.psum(squares_local, "path")
    path_rms = jnp.sqrt(summed / (scores.shape[1] * lax.axis_size("path")) + EPSILON)
    return (coefficients, velocity, scores, path_rms)


F32, BF16 = jnp.float32, jnp.bfloat16
TURN_PARTS = (6.28125, 0.001935482025146484, -1.748455600074e-07)
COS_TERMS = (1.0, -0.49999988079071045, 0.04166648909449577, -0.00138877984136343, 2.4769791707512923e-05, -2.707819533043221e-07, 1.7242244298998344e-09)
KEYS = 128
CHUNK = 256


def nt(left, right):
    return lax.dot_general(left, right, (((1,), (1,)), ((), ())), preferred_element_type=F32)


def nn(left, right):
    return lax.dot_general(left, right, (((1,), (0,)), ((), ())), preferred_element_type=F32)


def split(value, pieces):
    parts = []
    for _ in range(pieces):
        part = value.astype(BF16)
        parts.append(part)
        value = value - part.astype(F32)
    return parts


def stacked(value, pieces):
    return jnp.concatenate(split(value, pieces), axis=0)


def weighted(weights, tile, dot):
    rows = weights.shape[0]
    high, low = split(tile, 2)
    parts = stacked(weights, 2)
    both = dot(parts, high)
    return both[:rows] + both[rows:] + dot(parts[:rows], low)


def exactly(value, ones):
    rows = value.shape[0]
    thrice = nn(stacked(value, 3), ones)
    return thrice[:rows] + thrice[rows : 2 * rows] + thrice[2 * rows :]


def column_norms(rows):
    widened = rows.astype(F32)
    return jnp.sum(widened * widened, axis=1, keepdims=True)


def row_norms(rows):
    widened = rows.astype(F32)
    high, low = split(widened * widened, 2)
    ones = jnp.ones((16, rows.shape[1]), BF16)
    return (nt(ones, high) + nt(ones, low))[0:1]


def gaussian(left, left_norms, right, right_norms):
    return jnp.exp((2.0 * nt(left, right) - left_norms - right_norms) * (1.0 / left.shape[1]))


def cosine(angles):
    turns = jnp.round(angles * (1.0 / (2.0 * math.pi)))
    rest = angles
    for part in TURN_PARTS:
        rest = rest - turns * part
    square = rest * rest
    value = jnp.full_like(square, COS_TERMS[-1])
    for term in COS_TERMS[-2::-1]:
        value = value * square + term
    return value


def fused(
    n_blk, n_path,
    rec, coef, vel, targ, local, count, cand, freq, phase, weight,
    coef_out, vel_out, score_out, rms_out,
    xs, cand_in, partial, first_buf, second_buf, first_in, second_in, squares, local_pad,
    link_high, link_low, kx,
    x_send, x_recv, c_send, c_recv, p_send, p_recv, s_send, s_recv, q_send, q_recv,
):
    steps, cap = local.shape
    recs, width = rec.shape
    group = cand.shape[0]
    paths = coef.shape[0]
    slots = xs.shape[0] // n_blk
    total = xs.shape[0]
    root = math.sqrt(recs * n_blk)
    scale = SIGNAL / root
    me, my_path = lax.axis_index("blk"), lax.axis_index("path")

    def peer(by):
        return lax.rem(me + by, n_blk)

    def beside(by):
        return lax.rem(my_path + by, n_path)

    barrier = pltpu.get_barrier_semaphore()
    for by in range(1, n_blk):
        pl.semaphore_signal(barrier, inc=1, device_id={"blk": peer(by)}, device_id_type=pl.DeviceIdType.MESH)
    for by in range(1, n_path):
        pl.semaphore_signal(barrier, inc=1, device_id={"path": beside(by)}, device_id_type=pl.DeviceIdType.MESH)

    def remote(src, dst, send, recv, target):
        return pltpu.make_async_remote_copy(
            src_ref=src, dst_ref=dst, send_sem=send, recv_sem=recv,
            device_id=target, device_id_type=pl.DeviceIdType.MESH,
        )

    local_pad[...] = jnp.zeros_like(local_pad)
    local_pad[0:steps, 0:cap] = local[...].astype(F32)
    turned = jnp.transpose(local_pad[...])
    picked = jnp.concatenate(
        [turned[0:cap, t : t + 1] for t in range(steps)]
        + [jnp.full((slots - steps * cap, 1), -1.0, F32)],
        axis=0,
    )
    lanes = lax.broadcasted_iota(jnp.int32, (slots, recs), 1).astype(F32)
    chosen = (picked == lanes).astype(BF16)
    high_digit = jnp.floor(picked * (1.0 / 32.0))
    low_digit = picked - 32.0 * high_digit
    lane = lax.broadcasted_iota(jnp.int32, (slots, KEYS), 1)
    digits = jnp.where(lane == 0, high_digit, jnp.where(lane == 1, low_digit, 0.0))
    mine = nn(chosen, rec[...]).astype(BF16)
    block = pl.ds(pl.multiple_of(me * slots, slots), slots)
    xs[block, 0:width] = mine
    xs[block, width : width + KEYS] = digits.astype(BF16)

    pl.semaphore_wait(barrier, n_blk - 1 + n_path - 1)
    sends = []
    for by in range(1, n_blk):
        copy = remote(xs.at[block], xs.at[block], x_send.at[by], x_recv.at[by], {"blk": peer(by)})
        copy.start()
        sends.append(copy)
    cand_copy = remote(cand, cand_in, c_send, c_recv, {"blk": peer(1)})
    cand_copy.start()
    sends.append(cand_copy)

    start, speed0 = coef[...], vel[...]
    base = (start + geometric(1, steps) * speed0) * scale
    rec_norms = column_norms(rec[...])
    mine_norms = column_norms(mine)

    def base_values(rows):
        norms = row_norms(rows)
        value = jnp.zeros((paths, group), F32)
        for c in range(0, recs, CHUNK):
            tile = gaussian(rec[c : c + CHUNK, :], rec_norms[c : c + CHUNK], rows, norms)
            value = value + weighted(base[:, c : c + CHUNK], tile, nn)
        return value, gaussian(mine, mine_norms, rows, norms)

    feats = freq.shape[1]
    amplitude = weight[...] * math.sqrt(2.0 * SIGNAL / feats)
    first = jnp.zeros((paths, group), F32)
    for c in range(0, feats, CHUNK):
        part = slice(c, c + CHUNK)
        angles = nn(cand[...], freq[:, part]) * math.sqrt(2.0) + phase[:, part]
        first = first + weighted(amplitude[:, part], cosine(angles), nt)
    value, near = base_values(cand[...])
    first_buf[...] = first + value
    kx[:, 0:group] = near

    for by in range(1, n_blk):
        source = pl.ds(pl.multiple_of(peer(n_blk - by) * slots, slots), slots)
        remote(xs.at[source], xs.at[source], x_send.at[by], x_recv.at[by], {"blk": peer(by)}).wait_recv()
    points = xs[:, 0:width]
    point_digits = xs[:, width : width + KEYS]
    digit_lane = lax.broadcasted_iota(jnp.int32, (16, KEYS), 1)
    digit_worth = jnp.where(digit_lane == 0, 32.0, jnp.where(digit_lane == 1, 1.0, 0.0)).astype(BF16)
    place_row = lax.broadcasted_iota(jnp.int32, (1, total), 1).astype(F32)
    place_col = lax.broadcasted_iota(jnp.int32, (total, 1), 0).astype(F32)
    owner_row = jnp.floor((place_row + 0.5) * (1.0 / slots))
    owner_col = jnp.floor((place_col + 0.5) * (1.0 / slots))
    step_row = jnp.floor((place_row - slots * owner_row + 0.5) * (1.0 / cap))
    step_col = jnp.floor((place_col - slots * owner_col + 0.5) * (1.0 / cap))
    key_row = nt(digit_worth, point_digits)[0:1] + recs * owner_row
    spread = point_digits.astype(F32)
    key_col = 32.0 * spread[:, 0:1] + spread[:, 1:2] + recs * owner_col
    point_norms = row_norms(points)

    def by_step(step, values):
        out = jnp.zeros_like(step)
        for t, entry in enumerate(values):
            out = jnp.where(step == t, entry, out)
        return out

    me_first = (me * recs).astype(F32)
    held = jnp.concatenate([start, speed0], axis=0)
    sums = jnp.zeros((2 * paths, total), F32)
    owed = jnp.zeros((paths, total), F32)
    for c in range(0, recs, CHUNK):
        part = slice(c, c + CHUNK)
        ids = lax.broadcasted_iota(jnp.int32, (CHUNK, 1), 0).astype(F32) + (me_first + c)
        here = (ids == key_row).astype(F32)
        tile = gaussian(rec[part, :], rec_norms[part], points, point_norms) * scale + NOISE * here
        sums = sums + weighted(held[:, part], tile, nn)
        owed = owed + exactly(targ[:, part], here.astype(BF16))
    ahead = by_step(step_row, [geometric(1, t) for t in range(steps)])
    partial[me] = sums[:paths] + ahead * sums[paths:] - owed
    for by in range(1, n_blk):
        copy = remote(partial.at[me], partial.at[me], p_send.at[by], p_recv.at[by], {"blk": peer(by)})
        copy.start()
        sends.append(copy)

    for c in range(0, total, 128):
        part = slice(c, c + 128)
        same = (key_col[part] == key_row).astype(F32)
        tile = gaussian(points[part], column_norms(points[part]), points, point_norms) * scale + NOISE * same
        factor = by_step(
            step_row - step_col[part] - 1.0, [geometric(0, d) for d in range(steps - 1)]
        )
        factor = jnp.where(step_row < steps, factor, 0.0)
        high, low = split(tile * factor, 2)
        link_high[part, :] = high
        link_low[part, :] = low
    cand_copy.wait_recv()
    value, near = base_values(cand_in[...])
    second_buf[...] = value
    kx[:, group : 2 * group] = near
    live = jnp.zeros((1, total), F32)
    for t in range(steps):
        for o in range(n_blk):
            begin = float(o * slots + t * cap)
            upto = begin + count[t, o].astype(F32)
            live = jnp.where((place_row >= begin) & (place_row < upto), -RATE, live)
    select = (
        lax.broadcasted_iota(jnp.int32, (total, slots), 0)
        == lax.broadcasted_iota(jnp.int32, (total, slots), 1) + me * slots
    ).astype(BF16)

    for by in range(1, n_blk):
        source = peer(n_blk - by)
        remote(partial.at[source], partial.at[source], p_send.at[by], p_recv.at[by], {"blk": peer(by)}).wait_recv()
    gradient = partial[0]
    for o in range(1, n_blk):
        gradient = gradient + partial[o]
    moves = gradient * live
    for _ in range(steps - 1):
        parts = stacked(moves, 2)
        both = nn(parts, link_high[...])
        acted = both[:paths] + both[paths:] + nn(parts[:paths], link_low[...])
        moves = (gradient + acted) * live
    shift = moves * by_step(step_row, [geometric(0, steps - 1 - t) for t in range(steps)])
    kick = moves * by_step(step_row, [MOMENTUM ** (steps - 1 - t) for t in range(steps)])
    ours = exactly(jnp.concatenate([shift, kick], axis=0), select)

    late = weighted(ours[:paths] * scale, kx[...], nn)
    first_buf[...] = first_buf[...] + late[:, 0:group]
    second_buf[...] = second_buf[...] + late[:, group : 2 * group]
    first_copy = remote(first_buf, first_in, s_send.at[0], s_recv.at[0], {"blk": peer(2)})
    second_copy = remote(second_buf, second_in, s_send.at[1], s_recv.at[1], {"blk": peer(1)})
    first_copy.start()
    second_copy.start()
    sends += [first_copy, second_copy]
    added = exactly(ours, chosen)
    coef_out[...] = start + geometric(1, steps) * speed0 + added[:paths]
    vel_out[...] = MOMENTUM**steps * speed0 + added[paths:]
    first_copy.wait_recv()
    second_copy.wait_recv()
    scores = first_in[...] + second_in[...]
    score_out[...] = scores
    squares[my_path] = jnp.broadcast_to(jnp.sum(scores * scores, axis=0, keepdims=True), (8, group))
    for by in range(1, n_path):
        copy = remote(squares.at[my_path], squares.at[my_path], q_send.at[by], q_recv.at[by], {"path": beside(by)})
        copy.start()
        sends.append(copy)
    for by in range(1, n_path):
        source = beside(n_path - by)
        remote(squares.at[source], squares.at[source], q_send.at[by], q_recv.at[by], {"path": beside(by)}).wait_recv()
    summed = squares[0]
    for z in range(1, n_path):
        summed = summed + squares[z]
    rms_out[...] = jnp.sqrt(summed * (1.0 / (paths * n_path)) + EPSILON)[0:1]
    for copy in sends:
        copy.wait_send()


def fused_shards(
    n_blk, n_path,
    records, coefficients, velocity, targets, block_local, block_count,
    candidates, frequencies, phases, prior_weight,
):
    steps, cap = block_local.shape
    recs, width = records.shape
    group, paths = candidates.shape[0], coefficients.shape[1]
    slots = -(-(steps * cap + 1) // 16) * 16
    total = n_blk * slots
    vmem = pl.BlockSpec(memory_space=pltpu.VMEM)
    outs = pl.pallas_call(
        functools.partial(fused, n_blk, n_path),
        out_shape=(
            jax.ShapeDtypeStruct((paths, recs), F32),
            jax.ShapeDtypeStruct((paths, recs), F32),
            jax.ShapeDtypeStruct((paths, group), F32),
            jax.ShapeDtypeStruct((1, group), F32),
        ),
        in_specs=[vmem] * 5 + [pl.BlockSpec(memory_space=pltpu.SMEM)] + [vmem] * 4,
        out_specs=(vmem,) * 4,
        scratch_shapes=[
            pltpu.VMEM((total, width + KEYS), BF16),
            pltpu.VMEM((group, width), BF16),
            pltpu.VMEM((n_blk, paths, total), F32),
            pltpu.VMEM((paths, group), F32),
            pltpu.VMEM((paths, group), F32),
            pltpu.VMEM((paths, group), F32),
            pltpu.VMEM((paths, group), F32),
            pltpu.VMEM((n_path, 8, group), F32),
            pltpu.VMEM((8, 128), F32),
            pltpu.VMEM((total, total), BF16),
            pltpu.VMEM((total, total), BF16),
            pltpu.VMEM((slots, 2 * group), F32),
            pltpu.SemaphoreType.DMA((n_blk,)),
            pltpu.SemaphoreType.DMA((n_blk,)),
            pltpu.SemaphoreType.DMA,
            pltpu.SemaphoreType.DMA,
            pltpu.SemaphoreType.DMA((n_blk,)),
            pltpu.SemaphoreType.DMA((n_blk,)),
            pltpu.SemaphoreType.DMA((2,)),
            pltpu.SemaphoreType.DMA((2,)),
            pltpu.SemaphoreType.DMA((n_path,)),
            pltpu.SemaphoreType.DMA((n_path,)),
        ],
        compiler_params=pltpu.CompilerParams(
            collective_id=0, has_side_effects=True, vmem_limit_bytes=48 * 1024 * 1024
        ),
    )(
        records, coefficients.T, velocity.T, targets.T, block_local, block_count,
        candidates, frequencies, phases.reshape(1, -1), prior_weight.T,
    )
    return (outs[0].T, outs[1].T, outs[2].T, outs[3].reshape(-1))


def solution(mesh):

    n_blk, n_path = mesh.shape["blk"], mesh.shape["path"]
    body = functools.partial(fused_shards, n_blk, n_path) if n_blk <= 16 else shards
    return jax.shard_map(
        body,
        mesh=mesh,
        in_specs=(
            P("blk", None),
            P("blk", "path"),
            P("blk", "path"),
            P("blk", "path"),
            P(None, "blk"),
            P(),
            P("blk", None),
            P(),
            P(),
            P(None, "path"),
        ),
        out_specs=(P("blk", "path"), P("blk", "path"), P("blk", "path"), P("blk")),
        check_vma=False,
    )
```

```python
import functools
import math

import jax
import jax.numpy as jnp
from jax import lax
from jax.experimental import pallas as pl
from jax.experimental.pallas import tpu as pltpu
from jax.sharding import PartitionSpec as P

NOISE = 0.5
MOMENTUM = 0.9
RATE = 0.3
EPSILON = 1e-06
SIGNAL = 9.0


def passed_along(shard, axis, by):
    length = lax.axis_size(axis)
    return lax.ppermute(shard, axis, [(i, (i + by) % length) for i in range(length)])


def square_norms(row_block):
    widened = row_block.astype(jnp.float32)
    return jnp.sum(widened * widened, axis=-1)


def kernel_tile(left_rows, right_rows):
    dot_values = lax.dot_general(
        left_rows, right_rows, (((1,), (1,)), ((), ())), preferred_element_type=jnp.float32
    )
    distance = square_norms(left_rows)[:, None] + square_norms(right_rows)[None, :] - 2.0 * dot_values
    return SIGNAL * jnp.exp(-distance / left_rows.shape[1])


def product(left, right):
    return jnp.dot(left, right, precision=lax.Precision.HIGHEST)


def prior_values(cand_rows, frequencies, phases, prior_weight):
    angles = (
        jnp.dot(cand_rows, frequencies, preferred_element_type=jnp.float32) * math.sqrt(2.0)
        + phases[None, :]
    )
    features = math.sqrt(2.0 * SIGNAL / frequencies.shape[1]) * jnp.cos(angles)
    return product(features, prior_weight)


def geometric(first, last):
    return sum(MOMENTUM**i for i in range(first, last + 1))


def shards(
    records,
    coefficients,
    velocity,
    targets,
    block_local,
    block_count,
    candidates,
    frequencies,
    phases,
    prior_weight,
):
    n_blk = lax.axis_size("blk")
    record_total = records.shape[0] * n_blk
    root_count = jnp.sqrt(jnp.float32(record_total))
    steps, cap = block_local.shape
    own = lax.axis_index("blk")
    neighbour = passed_along(candidates, "blk", 1)
    picked = block_local.reshape(-1)
    gathered = lax.all_gather(records[picked], "blk", axis=0)
    ids = lax.all_gather(picked, "blk", axis=0) + (
        jnp.arange(n_blk, dtype=jnp.int32) * records.shape[0]
    )[:, None]
    rows, keys, partial = [], [], []
    for t in range(steps):
        part = slice(t * cap, (t + 1) * cap)
        rows.append(gathered[:, part].reshape(n_blk * cap, -1))
        keys.append(ids[:, part].reshape(-1))
        held = coefficients + geometric(1, t) * velocity
        local = product(kernel_tile(rows[t], records), held) / root_count
        mine = NOISE * held[block_local[t]] - targets[block_local[t]]
        before = lax.dynamic_slice_in_dim(local, own * cap, cap, 0)
        partial.append(lax.dynamic_update_slice_in_dim(local, before + mine, own * cap, 0))
    whole = lax.psum(jnp.stack(partial), "blk")
    moves = []
    for t in range(steps):
        gradient = whole[t]
        for s in range(t):
            link = kernel_tile(rows[t], rows[s]) / root_count + NOISE * (
                keys[t][:, None] == keys[s][None, :]
            ).astype(jnp.float32)
            gradient = gradient + geometric(0, t - 1 - s) * product(link, moves[s])
        live = (jnp.arange(cap, dtype=jnp.int32)[None, :] < block_count[t][:, None]).reshape(-1)
        moves.append(jnp.where(live[:, None], -RATE * gradient, 0.0))
    mine = [lax.dynamic_slice_in_dim(m, own * cap, cap, 0) for m in moves]
    speed = jnp.concatenate([MOMENTUM ** (steps - 1 - s) * m for s, m in enumerate(mine)])
    shift = jnp.concatenate([geometric(0, steps - 1 - s) * m for s, m in enumerate(mine)])
    both = jnp.concatenate(
        [
            coefficients + geometric(1, steps) * velocity,
            MOMENTUM**steps * velocity,
        ],
        axis=1,
    )
    both = both.at[picked].add(jnp.concatenate([shift, speed], axis=1))
    width = coefficients.shape[1]
    coefficients, velocity = both[:, :width], both[:, width:]
    own_sum = product(kernel_tile(candidates, records), coefficients)
    next_sum = product(kernel_tile(neighbour, records), coefficients)
    first_part = prior_values(candidates, frequencies, phases, prior_weight) + own_sum / root_count
    scores = passed_along(first_part, "blk", 2) + passed_along(next_sum / root_count, "blk", 1)
    squares_local = jnp.sum(scores * scores, axis=1)
    summed = lax.psum(squares_local, "path")
    path_rms = jnp.sqrt(summed / (scores.shape[1] * lax.axis_size("path")) + EPSILON)
    return (coefficients, velocity, scores, path_rms)


F32, BF16 = jnp.float32, jnp.bfloat16
TURN_PARTS = (6.28125, 0.001935482025146484, -1.748455600074e-07)
COS_TERMS = (1.0, -0.49999988079071045, 0.04166648909449577, -0.00138877984136343, 2.4769791707512923e-05, -2.707819533043221e-07, 1.7242244298998344e-09)
KEYS = 128
CHUNK = 256


def nt(left, right):
    return lax.dot_general(left, right, (((1,), (1,)), ((), ())), preferred_element_type=F32)


def nn(left, right):
    return lax.dot_general(left, right, (((1,), (0,)), ((), ())), preferred_element_type=F32)


def split(value, pieces):
    parts = []
    for _ in range(pieces):
        part = value.astype(BF16)
        parts.append(part)
        value = value - part.astype(F32)
    return parts


def stacked(value, pieces):
    return jnp.concatenate(split(value, pieces), axis=0)


def weighted(weights, tile, dot):
    rows = weights.shape[0]
    high, low = split(tile, 2)
    parts = stacked(weights, 2)
    both = dot(parts, high)
    return both[:rows] + both[rows:] + dot(parts[:rows], low)


def exactly(value, ones):
    rows = value.shape[0]
    thrice = nn(stacked(value, 3), ones)
    return thrice[:rows] + thrice[rows : 2 * rows] + thrice[2 * rows :]


def column_norms(rows):
    widened = rows.astype(F32)
    return jnp.sum(widened * widened, axis=1, keepdims=True)


def as_lanes(columns):
    rows = columns[0].shape[0]
    lane = lax.broadcasted_iota(jnp.int32, (rows, KEYS), 1)
    out = jnp.zeros((rows, KEYS), F32)
    for at, column in enumerate(columns):
        out = jnp.where(lane == at, column.astype(F32), out)
    return out.astype(BF16)


def row_norms(rows):
    return nt(jnp.ones((16, KEYS), BF16), as_lanes(split(column_norms(rows), 3)))[0:1]


def gaussian(left, left_norms, right, right_norms):
    rate = math.log2(math.e) / left.shape[1]
    return jnp.exp2(nt(left, right) * (2.0 * rate) - left_norms * rate - right_norms * rate)


def cosine(angles):
    turns = jnp.round(angles * (1.0 / (2.0 * math.pi)))
    rest = angles
    for part in TURN_PARTS:
        rest = rest - turns * part
    square = rest * rest
    value = jnp.full_like(square, COS_TERMS[-1])
    for term in COS_TERMS[-2::-1]:
        value = value * square + term
    return value


def fused(
    n_blk, n_path,
    rec_hbm, coef_hbm, vel_hbm, targ_hbm, local_hbm, count_hbm, cand_hbm, freq_hbm, phase_hbm, weight_hbm,
    coef_out, vel_out, score_out, rms_out,
    xs, cand_in, partial, first_buf, second_buf, first_in, second_in, squares, local_pad,
    link_high, link_low, kx,
    rec, coef, vel, targ, local, count, cand, freq, phase, weight, loaded,
    x_send, x_recv, c_send, c_recv, p_send, p_recv, s_send, s_recv, q_send, q_recv,
):
    steps, cap = local.shape
    recs, width = rec.shape
    group = cand.shape[0]
    paths = coef.shape[0]
    slots = xs.shape[0] // n_blk
    total = xs.shape[0]
    root = math.sqrt(recs * n_blk)
    scale = SIGNAL / root
    fetched = [
        (local_hbm, local), (rec_hbm, rec), (cand_hbm, cand), (coef_hbm, coef), (vel_hbm, vel),
        (targ_hbm, targ), (weight_hbm, weight), (phase_hbm, phase), (freq_hbm, freq), (count_hbm, count),
    ]
    fetches = [pltpu.make_async_copy(a, b, loaded.at[i]) for i, (a, b) in enumerate(fetched)]
    for fetch in fetches:
        fetch.start()
    me, my_path = lax.axis_index("blk"), lax.axis_index("path")

    def peer(by):
        return lax.rem(me + by, n_blk)

    def beside(by):
        return lax.rem(my_path + by, n_path)

    barrier = pltpu.get_barrier_semaphore()
    for by in range(1, n_blk):
        pl.semaphore_signal(barrier, inc=1, device_id={"blk": peer(by)}, device_id_type=pl.DeviceIdType.MESH)
    for by in range(1, n_path):
        pl.semaphore_signal(barrier, inc=1, device_id={"path": beside(by)}, device_id_type=pl.DeviceIdType.MESH)

    def remote(src, dst, send, recv, target):
        return pltpu.make_async_remote_copy(
            src_ref=src, dst_ref=dst, send_sem=send, recv_sem=recv,
            device_id=target, device_id_type=pl.DeviceIdType.MESH,
        )

    local_pad[...] = jnp.zeros_like(local_pad)
    fetches[0].wait()
    local_pad[0:steps, 0:cap] = local[...].astype(F32)
    turned = jnp.transpose(local_pad[...])
    picked = jnp.concatenate(
        [turned[0:cap, t : t + 1] for t in range(steps)]
        + [jnp.full((slots - steps * cap, 1), -1.0, F32)],
        axis=0,
    )
    lanes = lax.broadcasted_iota(jnp.int32, (slots, recs), 1).astype(F32)
    chosen = (picked == lanes).astype(BF16)
    high_digit = jnp.floor(picked * (1.0 / 32.0))
    low_digit = picked - 32.0 * high_digit
    fetches[1].wait()
    mine = nn(chosen, rec[...]).astype(BF16)
    mine_norms = column_norms(mine)
    block = pl.ds(pl.multiple_of(me * slots, slots), slots)
    xs[block, 0:width] = mine
    xs[block, width : width + KEYS] = as_lanes([high_digit, low_digit] + split(mine_norms, 3))

    pl.semaphore_wait(barrier, n_blk - 1 + n_path - 1)
    sends = []
    for by in range(1, n_blk):
        copy = remote(xs.at[block], xs.at[block], x_send.at[by], x_recv.at[by], {"blk": peer(by)})
        copy.start()
        sends.append(copy)
    fetches[2].wait()
    cand_copy = remote(cand, cand_in, c_send, c_recv, {"blk": peer(1)})
    cand_copy.start()
    sends.append(cand_copy)

    for fetch in fetches[3:]:
        fetch.wait()
    start, speed0 = coef[...], vel[...]
    at_mine = jnp.concatenate([start, speed0, targ[...]], axis=0)
    thrice = nt(stacked(at_mine, 3), chosen)
    at_mine = thrice[: 3 * paths] + thrice[3 * paths : 6 * paths] + thrice[6 * paths :]
    select = (
        lax.broadcasted_iota(jnp.int32, (total, slots), 0)
        == lax.broadcasted_iota(jnp.int32, (total, slots), 1) + me * slots
    ).astype(BF16)
    base = (start + geometric(1, steps) * speed0) * scale
    rec_norms = column_norms(rec[...])

    def base_values(rows):
        norms = row_norms(rows)
        value = jnp.zeros((paths, group), F32)
        for c in range(0, recs, CHUNK):
            tile = gaussian(rec[c : c + CHUNK, :], rec_norms[c : c + CHUNK], rows, norms)
            value = value + weighted(base[:, c : c + CHUNK], tile, nn)
        return value, gaussian(mine, mine_norms, rows, norms)

    feats = freq.shape[1]
    amplitude = weight[...] * math.sqrt(2.0 * SIGNAL / feats)
    first = jnp.zeros((paths, group), F32)
    for c in range(0, feats, CHUNK):
        part = slice(c, c + CHUNK)
        angles = nn(cand[...], freq[:, part]) * math.sqrt(2.0) + phase[:, part]
        first = first + weighted(amplitude[:, part], cosine(angles), nt)
    value, near = base_values(cand[...])
    first_buf[...] = first + value
    kx[:, 0:group] = near

    for by in range(1, n_blk):
        source = pl.ds(pl.multiple_of(peer(n_blk - by) * slots, slots), slots)
        remote(xs.at[source], xs.at[source], x_send.at[by], x_recv.at[by], {"blk": peer(by)}).wait_recv()
    points = xs[:, 0:width]
    point_digits = xs[:, width : width + KEYS]
    digit_lane = lax.broadcasted_iota(jnp.int32, (16, KEYS), 1)
    digit_line = lax.broadcasted_iota(jnp.int32, (16, KEYS), 0)
    digit_worth = jnp.where(digit_lane == 0, 32.0, jnp.where(digit_lane == 1, 1.0, 0.0))
    norm_worth = jnp.where((digit_lane >= 2) & (digit_lane < 5), 1.0, 0.0)
    worth = jnp.where(digit_line == 0, digit_worth, norm_worth).astype(BF16)
    place_row = lax.broadcasted_iota(jnp.int32, (1, total), 1).astype(F32)
    place_col = lax.broadcasted_iota(jnp.int32, (total, 1), 0).astype(F32)
    owner_row = jnp.floor((place_row + 0.5) * (1.0 / slots))
    owner_col = jnp.floor((place_col + 0.5) * (1.0 / slots))
    step_row = jnp.floor((place_row - slots * owner_row + 0.5) * (1.0 / cap))
    step_col = jnp.floor((place_col - slots * owner_col + 0.5) * (1.0 / cap))
    read = nt(worth, point_digits)
    key_row, point_norms = read[0:1] + recs * owner_row, read[1:2]
    spread = point_digits.astype(F32)
    key_col = 32.0 * spread[:, 0:1] + spread[:, 1:2] + recs * owner_col
    norms_col = spread[:, 2:3] + spread[:, 3:4] + spread[:, 4:5]

    def by_step(step, values):
        out = jnp.zeros_like(step)
        for t, entry in enumerate(values):
            out = jnp.where(step == t, entry, out)
        return out

    held = jnp.concatenate([start, speed0], axis=0) * scale
    sums = jnp.zeros((2 * paths, total), F32)
    for c in range(0, recs, CHUNK):
        part = slice(c, c + CHUNK)
        tile = gaussian(rec[part, :], rec_norms[part], points, point_norms)
        sums = sums + weighted(held[:, part], tile, nn)
    placed = nt(stacked(at_mine, 3), select)
    placed = placed[: 3 * paths] + placed[3 * paths : 6 * paths] + placed[6 * paths :]
    sums = sums + NOISE * placed[: 2 * paths]
    owed = placed[2 * paths :]
    ahead = by_step(step_row, [geometric(1, t) for t in range(steps)])
    partial[me] = sums[:paths] + ahead * sums[paths:] - owed
    for by in range(1, n_blk):
        copy = remote(partial.at[me], partial.at[me], p_send.at[by], p_recv.at[by], {"blk": peer(by)})
        copy.start()
        sends.append(copy)

    for c in range(0, total, 128):
        part = slice(c, c + 128)
        same = (key_col[part] == key_row).astype(F32)
        tile = gaussian(points[part], norms_col[part], points, point_norms) * scale + NOISE * same
        factor = by_step(
            step_row - step_col[part] - 1.0, [geometric(0, d) for d in range(steps - 1)]
        )
        factor = jnp.where(step_row < steps, factor, 0.0)
        high, low = split(tile * factor, 2)
        link_high[part, :] = high
        link_low[part, :] = low
    cand_copy.wait_recv()
    value, near = base_values(cand_in[...])
    second_buf[...] = value
    kx[:, group : 2 * group] = near
    live = jnp.zeros((1, total), F32)
    for t in range(steps):
        for o in range(n_blk):
            begin = float(o * slots + t * cap)
            upto = begin + count[t, o].astype(F32)
            live = jnp.where((place_row >= begin) & (place_row < upto), -RATE, live)
    for by in range(1, n_blk):
        source = peer(n_blk - by)
        remote(partial.at[source], partial.at[source], p_send.at[by], p_recv.at[by], {"blk": peer(by)}).wait_recv()
    gradient = partial[0]
    for o in range(1, n_blk):
        gradient = gradient + partial[o]
    moves = gradient * live
    for _ in range(steps - 1):
        parts = stacked(moves, 2)
        both = nn(parts, link_high[...])
        acted = both[:paths] + both[paths:] + nn(parts[:paths], link_low[...])
        moves = (gradient + acted) * live
    shift = moves * by_step(step_row, [geometric(0, steps - 1 - t) for t in range(steps)])
    kick = moves * by_step(step_row, [MOMENTUM ** (steps - 1 - t) for t in range(steps)])
    ours = exactly(jnp.concatenate([shift, kick], axis=0), select)

    late = weighted(ours[:paths] * scale, kx[...], nn)
    first_buf[...] = first_buf[...] + late[:, 0:group]
    second_buf[...] = second_buf[...] + late[:, group : 2 * group]
    first_copy = remote(first_buf, first_in, s_send.at[0], s_recv.at[0], {"blk": peer(2)})
    second_copy = remote(second_buf, second_in, s_send.at[1], s_recv.at[1], {"blk": peer(1)})
    first_copy.start()
    second_copy.start()
    sends += [first_copy, second_copy]
    added = exactly(ours, chosen)
    coef_out[...] = start + geometric(1, steps) * speed0 + added[:paths]
    vel_out[...] = MOMENTUM**steps * speed0 + added[paths:]
    first_copy.wait_recv()
    second_copy.wait_recv()
    scores = first_in[...] + second_in[...]
    score_out[...] = scores
    squares[my_path] = jnp.broadcast_to(jnp.sum(scores * scores, axis=0, keepdims=True), (8, group))
    for by in range(1, n_path):
        copy = remote(squares.at[my_path], squares.at[my_path], q_send.at[by], q_recv.at[by], {"path": beside(by)})
        copy.start()
        sends.append(copy)
    for by in range(1, n_path):
        source = beside(n_path - by)
        remote(squares.at[source], squares.at[source], q_send.at[by], q_recv.at[by], {"path": beside(by)}).wait_recv()
    summed = squares[0]
    for z in range(1, n_path):
        summed = summed + squares[z]
    rms_out[...] = jnp.sqrt(summed * (1.0 / (paths * n_path)) + EPSILON)[0:1]
    for copy in sends:
        copy.wait_send()


def written(a, b, c, d, to_a, to_b, to_c, to_d, done):
    pairs = [(a, to_a), (b, to_b), (c, to_c), (d, to_d)]
    copies = [pltpu.make_async_copy(x, y, done.at[i]) for i, (x, y) in enumerate(pairs)]
    for copy in copies:
        copy.start()
    for copy in copies:
        copy.wait()


def fused_shards(
    n_blk, n_path,
    records, coefficients, velocity, targets, block_local, block_count,
    candidates, frequencies, phases, prior_weight,
):
    steps, cap = block_local.shape
    recs, width = records.shape
    group, paths = candidates.shape[0], coefficients.shape[1]
    slots = -(-(steps * cap + 1) // 16) * 16
    total = n_blk * slots
    vmem, hbm = pl.BlockSpec(memory_space=pltpu.VMEM), pl.BlockSpec(memory_space=pltpu.HBM)
    outs = pl.pallas_call(
        functools.partial(fused, n_blk, n_path),
        out_shape=(
            jax.ShapeDtypeStruct((paths, recs), F32),
            jax.ShapeDtypeStruct((paths, recs), F32),
            jax.ShapeDtypeStruct((paths, group), F32),
            jax.ShapeDtypeStruct((1, group), F32),
        ),
        in_specs=[hbm] * 10,
        out_specs=(vmem,) * 4,
        scratch_shapes=[
            pltpu.VMEM((total, width + KEYS), BF16),
            pltpu.VMEM((group, width), BF16),
            pltpu.VMEM((n_blk, paths, total), F32),
            pltpu.VMEM((paths, group), F32),
            pltpu.VMEM((paths, group), F32),
            pltpu.VMEM((paths, group), F32),
            pltpu.VMEM((paths, group), F32),
            pltpu.VMEM((n_path, 8, group), F32),
            pltpu.VMEM((8, 128), F32),
            pltpu.VMEM((total, total), BF16),
            pltpu.VMEM((total, total), BF16),
            pltpu.VMEM((slots, 2 * group), F32),
            pltpu.VMEM(records.shape, BF16),
            pltpu.VMEM((paths, recs), F32),
            pltpu.VMEM((paths, recs), F32),
            pltpu.VMEM((paths, recs), F32),
            pltpu.VMEM(block_local.shape, jnp.int32),
            pltpu.SMEM(block_count.shape, jnp.int32),
            pltpu.VMEM(candidates.shape, BF16),
            pltpu.VMEM(frequencies.shape, BF16),
            pltpu.VMEM((1, phases.shape[0]), F32),
            pltpu.VMEM((paths, phases.shape[0]), F32),
            pltpu.SemaphoreType.DMA((10,)),
            pltpu.SemaphoreType.DMA((n_blk,)),
            pltpu.SemaphoreType.DMA((n_blk,)),
            pltpu.SemaphoreType.DMA,
            pltpu.SemaphoreType.DMA,
            pltpu.SemaphoreType.DMA((n_blk,)),
            pltpu.SemaphoreType.DMA((n_blk,)),
            pltpu.SemaphoreType.DMA((2,)),
            pltpu.SemaphoreType.DMA((2,)),
            pltpu.SemaphoreType.DMA((n_path,)),
            pltpu.SemaphoreType.DMA((n_path,)),
        ],
        compiler_params=pltpu.CompilerParams(
            collective_id=0, has_side_effects=True, vmem_limit_bytes=60 * 1024 * 1024
        ),
    )(
        records, coefficients.T, velocity.T, targets.T, block_local, block_count,
        candidates, frequencies, phases.reshape(1, -1), prior_weight.T,
    )
    outs = pl.pallas_call(
        written,
        out_shape=[jax.ShapeDtypeStruct(o.shape, o.dtype) for o in outs],
        in_specs=[hbm] * 4,
        out_specs=[hbm] * 4,
        scratch_shapes=[pltpu.SemaphoreType.DMA((4,))],
        compiler_params=pltpu.CompilerParams(vmem_limit_bytes=60 * 1024 * 1024),
    )(*outs)
    return (outs[0].T, outs[1].T, outs[2].T, outs[3].reshape(-1))


def solution(mesh):

    n_blk, n_path = mesh.shape["blk"], mesh.shape["path"]
    body = functools.partial(fused_shards, n_blk, n_path) if n_blk <= 16 else shards
    return jax.shard_map(
        body,
        mesh=mesh,
        in_specs=(
            P("blk", None),
            P("blk", "path"),
            P("blk", "path"),
            P("blk", "path"),
            P(None, "blk"),
            P(),
            P("blk", None),
            P(),
            P(),
            P(None, "path"),
        ),
        out_specs=(P("blk", "path"), P("blk", "path"), P("blk", "path"), P("blk")),
        check_vma=False,
    )
```

```python
import functools
import math

import jax
import jax.numpy as jnp
from jax import lax
from jax.experimental import pallas as pl
from jax.experimental.pallas import tpu as pltpu
from jax.sharding import PartitionSpec as P

NOISE = 0.5
MOMENTUM = 0.9
RATE = 0.3
EPSILON = 1e-06
SIGNAL = 9.0


def passed_along(shard, axis, by):
    length = lax.axis_size(axis)
    return lax.ppermute(shard, axis, [(i, (i + by) % length) for i in range(length)])


def square_norms(row_block):
    widened = row_block.astype(jnp.float32)
    return jnp.sum(widened * widened, axis=-1)


def kernel_tile(left_rows, right_rows):
    dot_values = lax.dot_general(
        left_rows, right_rows, (((1,), (1,)), ((), ())), preferred_element_type=jnp.float32
    )
    distance = square_norms(left_rows)[:, None] + square_norms(right_rows)[None, :] - 2.0 * dot_values
    return SIGNAL * jnp.exp(-distance / left_rows.shape[1])


def product(left, right):
    return jnp.dot(left, right, precision=lax.Precision.HIGHEST)


def prior_values(cand_rows, frequencies, phases, prior_weight):
    angles = (
        jnp.dot(cand_rows, frequencies, preferred_element_type=jnp.float32) * math.sqrt(2.0)
        + phases[None, :]
    )
    features = math.sqrt(2.0 * SIGNAL / frequencies.shape[1]) * jnp.cos(angles)
    return product(features, prior_weight)


def geometric(first, last):
    return sum(MOMENTUM**i for i in range(first, last + 1))


def shards(
    records,
    coefficients,
    velocity,
    targets,
    block_local,
    block_count,
    candidates,
    frequencies,
    phases,
    prior_weight,
):
    n_blk = lax.axis_size("blk")
    record_total = records.shape[0] * n_blk
    root_count = jnp.sqrt(jnp.float32(record_total))
    steps, cap = block_local.shape
    own = lax.axis_index("blk")
    neighbour = passed_along(candidates, "blk", 1)
    picked = block_local.reshape(-1)
    gathered = lax.all_gather(records[picked], "blk", axis=0)
    ids = lax.all_gather(picked, "blk", axis=0) + (
        jnp.arange(n_blk, dtype=jnp.int32) * records.shape[0]
    )[:, None]
    rows, keys, partial = [], [], []
    for t in range(steps):
        part = slice(t * cap, (t + 1) * cap)
        rows.append(gathered[:, part].reshape(n_blk * cap, -1))
        keys.append(ids[:, part].reshape(-1))
        held = coefficients + geometric(1, t) * velocity
        local = product(kernel_tile(rows[t], records), held) / root_count
        mine = NOISE * held[block_local[t]] - targets[block_local[t]]
        before = lax.dynamic_slice_in_dim(local, own * cap, cap, 0)
        partial.append(lax.dynamic_update_slice_in_dim(local, before + mine, own * cap, 0))
    whole = lax.psum(jnp.stack(partial), "blk")
    moves = []
    for t in range(steps):
        gradient = whole[t]
        for s in range(t):
            link = kernel_tile(rows[t], rows[s]) / root_count + NOISE * (
                keys[t][:, None] == keys[s][None, :]
            ).astype(jnp.float32)
            gradient = gradient + geometric(0, t - 1 - s) * product(link, moves[s])
        live = (jnp.arange(cap, dtype=jnp.int32)[None, :] < block_count[t][:, None]).reshape(-1)
        moves.append(jnp.where(live[:, None], -RATE * gradient, 0.0))
    mine = [lax.dynamic_slice_in_dim(m, own * cap, cap, 0) for m in moves]
    speed = jnp.concatenate([MOMENTUM ** (steps - 1 - s) * m for s, m in enumerate(mine)])
    shift = jnp.concatenate([geometric(0, steps - 1 - s) * m for s, m in enumerate(mine)])
    both = jnp.concatenate(
        [
            coefficients + geometric(1, steps) * velocity,
            MOMENTUM**steps * velocity,
        ],
        axis=1,
    )
    both = both.at[picked].add(jnp.concatenate([shift, speed], axis=1))
    width = coefficients.shape[1]
    coefficients, velocity = both[:, :width], both[:, width:]
    own_sum = product(kernel_tile(candidates, records), coefficients)
    next_sum = product(kernel_tile(neighbour, records), coefficients)
    first_part = prior_values(candidates, frequencies, phases, prior_weight) + own_sum / root_count
    scores = passed_along(first_part, "blk", 2) + passed_along(next_sum / root_count, "blk", 1)
    squares_local = jnp.sum(scores * scores, axis=1)
    summed = lax.psum(squares_local, "path")
    path_rms = jnp.sqrt(summed / (scores.shape[1] * lax.axis_size("path")) + EPSILON)
    return (coefficients, velocity, scores, path_rms)


F32, BF16 = jnp.float32, jnp.bfloat16
TURN_PARTS = (6.28125, 0.001935482025146484, -1.748455600074e-07)
COS_TERMS = (1.0, -0.49999988079071045, 0.04166648909449577, -0.00138877984136343, 2.4769791707512923e-05, -2.707819533043221e-07, 1.7242244298998344e-09)
KEYS = 128
CHUNK = 256


def nt(left, right):
    return lax.dot_general(left, right, (((1,), (1,)), ((), ())), preferred_element_type=F32)


def nn(left, right):
    return lax.dot_general(left, right, (((1,), (0,)), ((), ())), preferred_element_type=F32)


def split(value, pieces):
    parts = []
    for _ in range(pieces):
        part = value.astype(BF16)
        parts.append(part)
        value = value - part.astype(F32)
    return parts


def stacked(value, pieces):
    return jnp.concatenate(split(value, pieces), axis=0)


def weighted(weights, tile, dot):
    rows = weights.shape[0]
    high, low = split(tile, 2)
    parts = stacked(weights, 2)
    both = dot(parts, high)
    return both[:rows] + both[rows:] + dot(parts[:rows], low)


def exactly(value, ones):
    rows = value.shape[0]
    thrice = nn(stacked(value, 3), ones)
    return thrice[:rows] + thrice[rows : 2 * rows] + thrice[2 * rows :]


def column_norms(rows):
    widened = rows.astype(F32)
    return jnp.sum(widened * widened, axis=1, keepdims=True)


def as_lanes(columns):
    rows = columns[0].shape[0]
    lane = lax.broadcasted_iota(jnp.int32, (rows, KEYS), 1)
    out = jnp.zeros((rows, KEYS), F32)
    for at, column in enumerate(columns):
        out = jnp.where(lane == at, column.astype(F32), out)
    return out.astype(BF16)


def row_norms(rows):
    return nt(jnp.ones((16, KEYS), BF16), as_lanes(split(column_norms(rows), 3)))[0:1]


def gaussian(left, left_norms, right, right_norms):
    rate = math.log2(math.e) / left.shape[1]
    return jnp.exp2(nt(left, right) * (2.0 * rate) - left_norms * rate - right_norms * rate)


def cosine(angles):
    turns = jnp.round(angles * (1.0 / (2.0 * math.pi)))
    rest = angles
    for part in TURN_PARTS:
        rest = rest - turns * part
    square = rest * rest
    value = jnp.full_like(square, COS_TERMS[-1])
    for term in COS_TERMS[-2::-1]:
        value = value * square + term
    return value


def fused(
    n_blk, n_path,
    rec_hbm, coef_hbm, vel_hbm, targ_hbm, local_hbm, count_hbm, cand_hbm, freq_hbm, phase_hbm, weight_hbm,
    coef_out, vel_out, score_out, rms_out,
    xs, cand_in, partial, first_buf, second_buf, first_in, second_in, squares, local_pad,
    link_high, link_low, kx,
    rec, coef, vel, targ, local, count, cand, freq, phase, weight, loaded,
    x_send, x_recv, c_send, c_recv, p_send, p_recv, s_send, s_recv, q_send, q_recv,
):
    steps, cap = local.shape
    recs, width = rec.shape
    group = cand.shape[0]
    paths = coef.shape[0]
    slots = xs.shape[0] // n_blk
    total = xs.shape[0]
    root = math.sqrt(recs * n_blk)
    scale = SIGNAL / root
    fetched = [
        (local_hbm, local), (rec_hbm, rec), (cand_hbm, cand), (coef_hbm, coef), (vel_hbm, vel),
        (targ_hbm, targ), (weight_hbm, weight), (phase_hbm, phase), (freq_hbm, freq), (count_hbm, count),
    ]
    fetches = [pltpu.make_async_copy(a, b, loaded.at[i]) for i, (a, b) in enumerate(fetched)]
    for fetch in fetches:
        fetch.start()
    me, my_path = lax.axis_index("blk"), lax.axis_index("path")

    def peer(by):
        return lax.rem(me + by, n_blk)

    def beside(by):
        return lax.rem(my_path + by, n_path)

    barrier = pltpu.get_barrier_semaphore()
    for by in range(1, n_blk):
        pl.semaphore_signal(barrier, inc=1, device_id={"blk": peer(by)}, device_id_type=pl.DeviceIdType.MESH)
    for by in range(1, n_path):
        pl.semaphore_signal(barrier, inc=1, device_id={"path": beside(by)}, device_id_type=pl.DeviceIdType.MESH)

    def remote(src, dst, send, recv, target):
        return pltpu.make_async_remote_copy(
            src_ref=src, dst_ref=dst, send_sem=send, recv_sem=recv,
            device_id=target, device_id_type=pl.DeviceIdType.MESH,
        )

    local_pad[...] = jnp.zeros_like(local_pad)
    fetches[0].wait()
    local_pad[0:steps, 0:cap] = local[...].astype(F32)
    turned = jnp.transpose(local_pad[...])
    picked = jnp.concatenate(
        [turned[0:cap, t : t + 1] for t in range(steps)]
        + [jnp.full((slots - steps * cap, 1), -1.0, F32)],
        axis=0,
    )
    lanes = lax.broadcasted_iota(jnp.int32, (slots, recs), 1).astype(F32)
    chosen = (picked == lanes).astype(BF16)
    high_digit = jnp.floor(picked * (1.0 / 32.0))
    low_digit = picked - 32.0 * high_digit
    fetches[1].wait()
    mine = nn(chosen, rec[...]).astype(BF16)
    mine_norms = column_norms(mine)
    block = pl.ds(pl.multiple_of(me * slots, slots), slots)
    xs[block, 0:width] = mine
    xs[block, width : width + KEYS] = as_lanes([high_digit, low_digit] + split(mine_norms, 3))

    pl.semaphore_wait(barrier, n_blk - 1 + n_path - 1)
    sends = []
    for by in range(1, n_blk):
        copy = remote(xs.at[block], xs.at[block], x_send.at[by], x_recv.at[by], {"blk": peer(by)})
        copy.start()
        sends.append(copy)
    fetches[2].wait()
    cand_copy = remote(cand, cand_in, c_send, c_recv, {"blk": peer(1)})
    cand_copy.start()
    sends.append(cand_copy)

    for fetch in fetches[3:]:
        fetch.wait()
    start, speed0 = coef[...], vel[...]
    at_mine = jnp.concatenate([start, speed0, targ[...]], axis=0)
    thrice = nt(stacked(at_mine, 3), chosen)
    at_mine = thrice[: 3 * paths] + thrice[3 * paths : 6 * paths] + thrice[6 * paths :]
    select = (
        lax.broadcasted_iota(jnp.int32, (total, slots), 0)
        == lax.broadcasted_iota(jnp.int32, (total, slots), 1) + me * slots
    ).astype(BF16)
    base = (start + geometric(1, steps) * speed0) * scale
    rec_norms = column_norms(rec[...])

    def base_values(rows):
        norms = row_norms(rows)
        value = jnp.zeros((paths, group), F32)
        for c in range(0, recs, CHUNK):
            tile = gaussian(rec[c : c + CHUNK, :], rec_norms[c : c + CHUNK], rows, norms)
            value = value + weighted(base[:, c : c + CHUNK], tile, nn)
        return value, gaussian(mine, mine_norms, rows, norms)

    feats = freq.shape[1]
    amplitude = weight[...] * math.sqrt(2.0 * SIGNAL / feats)
    first = jnp.zeros((paths, group), F32)
    for c in range(0, feats, CHUNK):
        part = slice(c, c + CHUNK)
        angles = nn(cand[...], freq[:, part]) * math.sqrt(2.0) + phase[:, part]
        first = first + weighted(amplitude[:, part], cosine(angles), nt)
    value, near = base_values(cand[...])
    first_buf[...] = first + value
    kx[:, 0:group] = near

    for by in range(1, n_blk):
        source = pl.ds(pl.multiple_of(peer(n_blk - by) * slots, slots), slots)
        remote(xs.at[source], xs.at[source], x_send.at[by], x_recv.at[by], {"blk": peer(by)}).wait_recv()
    points = xs[:, 0:width]
    point_digits = xs[:, width : width + KEYS]
    digit_lane = lax.broadcasted_iota(jnp.int32, (16, KEYS), 1)
    digit_line = lax.broadcasted_iota(jnp.int32, (16, KEYS), 0)
    digit_worth = jnp.where(digit_lane == 0, 32.0, jnp.where(digit_lane == 1, 1.0, 0.0))
    norm_worth = jnp.where((digit_lane >= 2) & (digit_lane < 5), 1.0, 0.0)
    worth = jnp.where(digit_line == 0, digit_worth, norm_worth).astype(BF16)
    place_row = lax.broadcasted_iota(jnp.int32, (1, total), 1).astype(F32)
    place_col = lax.broadcasted_iota(jnp.int32, (total, 1), 0).astype(F32)
    owner_row = jnp.floor((place_row + 0.5) * (1.0 / slots))
    owner_col = jnp.floor((place_col + 0.5) * (1.0 / slots))
    step_row = jnp.floor((place_row - slots * owner_row + 0.5) * (1.0 / cap))
    step_col = jnp.floor((place_col - slots * owner_col + 0.5) * (1.0 / cap))
    read = nt(worth, point_digits)
    key_row, point_norms = read[0:1] + recs * owner_row, read[1:2]
    spread = point_digits.astype(F32)
    key_col = 32.0 * spread[:, 0:1] + spread[:, 1:2] + recs * owner_col
    norms_col = spread[:, 2:3] + spread[:, 3:4] + spread[:, 4:5]

    def by_step(step, values):
        out = jnp.zeros_like(step)
        for t, entry in enumerate(values):
            out = jnp.where(step == t, entry, out)
        return out

    held = jnp.concatenate([start, speed0], axis=0) * scale
    sums = jnp.zeros((2 * paths, total), F32)
    for c in range(0, recs, CHUNK):
        part = slice(c, c + CHUNK)
        tile = gaussian(rec[part, :], rec_norms[part], points, point_norms)
        sums = sums + weighted(held[:, part], tile, nn)
    placed = nt(stacked(at_mine, 3), select)
    placed = placed[: 3 * paths] + placed[3 * paths : 6 * paths] + placed[6 * paths :]
    sums = sums + NOISE * placed[: 2 * paths]
    owed = placed[2 * paths :]
    ahead = by_step(step_row, [geometric(1, t) for t in range(steps)])
    partial[me] = sums[:paths] + ahead * sums[paths:] - owed
    for by in range(1, n_blk):
        copy = remote(partial.at[me], partial.at[me], p_send.at[by], p_recv.at[by], {"blk": peer(by)})
        copy.start()
        sends.append(copy)

    for c in range(0, total, 128):
        part = slice(c, c + 128)
        same = (key_col[part] == key_row).astype(F32)
        tile = gaussian(points[part], norms_col[part], points, point_norms) * scale + NOISE * same
        factor = by_step(
            step_row - step_col[part] - 1.0, [geometric(0, d) for d in range(steps - 1)]
        )
        factor = jnp.where(step_row < steps, factor, 0.0)
        high, low = split(tile * factor, 2)
        link_high[part, :] = high
        link_low[part, :] = low
    cand_copy.wait_recv()
    value, near = base_values(cand_in[...])
    second_buf[...] = value
    kx[:, group : 2 * group] = near
    live = jnp.zeros((1, total), F32)
    for t in range(steps):
        for o in range(n_blk):
            begin = float(o * slots + t * cap)
            upto = begin + count[t, o].astype(F32)
            live = jnp.where((place_row >= begin) & (place_row < upto), -RATE, live)
    for by in range(1, n_blk):
        source = peer(n_blk - by)
        remote(partial.at[source], partial.at[source], p_send.at[by], p_recv.at[by], {"blk": peer(by)}).wait_recv()
    gradient = partial[0]
    for o in range(1, n_blk):
        gradient = gradient + partial[o]
    moves = gradient * live
    for _ in range(steps - 1):
        parts = stacked(moves, 2)
        both = nn(parts, link_high[...])
        acted = both[:paths] + both[paths:] + nn(parts[:paths], link_low[...])
        moves = (gradient + acted) * live
    shift = moves * by_step(step_row, [geometric(0, steps - 1 - t) for t in range(steps)])
    kick = moves * by_step(step_row, [MOMENTUM ** (steps - 1 - t) for t in range(steps)])
    ours = exactly(jnp.concatenate([shift, kick], axis=0), select)

    late = weighted(ours[:paths] * scale, kx[...], nn)
    first_buf[...] = first_buf[...] + late[:, 0:group]
    second_buf[...] = second_buf[...] + late[:, group : 2 * group]
    first_copy = remote(first_buf, first_in, s_send.at[0], s_recv.at[0], {"blk": peer(2)})
    second_copy = remote(second_buf, second_in, s_send.at[1], s_recv.at[1], {"blk": peer(1)})
    first_copy.start()
    second_copy.start()
    sends += [first_copy, second_copy]
    added = exactly(ours, chosen)
    coef_out[...] = start + geometric(1, steps) * speed0 + added[:paths]
    vel_out[...] = MOMENTUM**steps * speed0 + added[paths:]
    first_copy.wait_recv()
    second_copy.wait_recv()
    scores = first_in[...] + second_in[...]
    score_out[...] = scores
    squares[my_path] = jnp.broadcast_to(jnp.sum(scores * scores, axis=0, keepdims=True), (8, group))
    for by in range(1, n_path):
        copy = remote(squares.at[my_path], squares.at[my_path], q_send.at[by], q_recv.at[by], {"path": beside(by)})
        copy.start()
        sends.append(copy)
    for by in range(1, n_path):
        source = beside(n_path - by)
        remote(squares.at[source], squares.at[source], q_send.at[by], q_recv.at[by], {"path": beside(by)}).wait_recv()
    summed = squares[0]
    for z in range(1, n_path):
        summed = summed + squares[z]
    rms_out[...] = jnp.sqrt(summed * (1.0 / (paths * n_path)) + EPSILON)[0:1]
    for copy in sends:
        copy.wait_send()


def written(a, b, c, d, to_a, to_b, to_c, to_d):
    to_a[...], to_b[...], to_c[...], to_d[...] = a[...], b[...], c[...], d[...]


def fused_shards(
    n_blk, n_path,
    records, coefficients, velocity, targets, block_local, block_count,
    candidates, frequencies, phases, prior_weight,
):
    steps, cap = block_local.shape
    recs, width = records.shape
    group, paths = candidates.shape[0], coefficients.shape[1]
    slots = -(-(steps * cap + 1) // 16) * 16
    total = n_blk * slots
    vmem, hbm = pl.BlockSpec(memory_space=pltpu.VMEM), pl.BlockSpec(memory_space=pltpu.HBM)
    outs = pl.pallas_call(
        functools.partial(fused, n_blk, n_path),
        out_shape=(
            jax.ShapeDtypeStruct((paths, recs), F32),
            jax.ShapeDtypeStruct((paths, recs), F32),
            jax.ShapeDtypeStruct((paths, group), F32),
            jax.ShapeDtypeStruct((1, group), F32),
        ),
        in_specs=[hbm] * 10,
        out_specs=(vmem,) * 4,
        scratch_shapes=[
            pltpu.VMEM((total, width + KEYS), BF16),
            pltpu.VMEM((group, width), BF16),
            pltpu.VMEM((n_blk, paths, total), F32),
            pltpu.VMEM((paths, group), F32),
            pltpu.VMEM((paths, group), F32),
            pltpu.VMEM((paths, group), F32),
            pltpu.VMEM((paths, group), F32),
            pltpu.VMEM((n_path, 8, group), F32),
            pltpu.VMEM((8, 128), F32),
            pltpu.VMEM((total, total), BF16),
            pltpu.VMEM((total, total), BF16),
            pltpu.VMEM((slots, 2 * group), F32),
            pltpu.VMEM(records.shape, BF16),
            pltpu.VMEM((paths, recs), F32),
            pltpu.VMEM((paths, recs), F32),
            pltpu.VMEM((paths, recs), F32),
            pltpu.VMEM(block_local.shape, jnp.int32),
            pltpu.SMEM(block_count.shape, jnp.int32),
            pltpu.VMEM(candidates.shape, BF16),
            pltpu.VMEM(frequencies.shape, BF16),
            pltpu.VMEM((1, phases.shape[0]), F32),
            pltpu.VMEM((paths, phases.shape[0]), F32),
            pltpu.SemaphoreType.DMA((10,)),
            pltpu.SemaphoreType.DMA((n_blk,)),
            pltpu.SemaphoreType.DMA((n_blk,)),
            pltpu.SemaphoreType.DMA,
            pltpu.SemaphoreType.DMA,
            pltpu.SemaphoreType.DMA((n_blk,)),
            pltpu.SemaphoreType.DMA((n_blk,)),
            pltpu.SemaphoreType.DMA((2,)),
            pltpu.SemaphoreType.DMA((2,)),
            pltpu.SemaphoreType.DMA((n_path,)),
            pltpu.SemaphoreType.DMA((n_path,)),
        ],
        compiler_params=pltpu.CompilerParams(
            collective_id=0, has_side_effects=True, vmem_limit_bytes=60 * 1024 * 1024
        ),
    )(
        records, coefficients.T, velocity.T, targets.T, block_local, block_count,
        candidates, frequencies, phases.reshape(1, -1), prior_weight.T,
    )
    outs = pl.pallas_call(
        written,
        out_shape=[jax.ShapeDtypeStruct(o.shape, o.dtype) for o in outs],
        in_specs=[vmem] * 4,
        out_specs=[vmem] * 4,
        compiler_params=pltpu.CompilerParams(vmem_limit_bytes=60 * 1024 * 1024),
    )(*outs)
    return (outs[0].T, outs[1].T, outs[2].T, outs[3].reshape(-1))


def solution(mesh):

    n_blk, n_path = mesh.shape["blk"], mesh.shape["path"]
    body = functools.partial(fused_shards, n_blk, n_path) if n_blk <= 16 else shards
    return jax.shard_map(
        body,
        mesh=mesh,
        in_specs=(
            P("blk", None),
            P("blk", "path"),
            P("blk", "path"),
            P("blk", "path"),
            P(None, "blk"),
            P(),
            P("blk", None),
            P(),
            P(),
            P(None, "path"),
        ),
        out_specs=(P("blk", "path"), P("blk", "path"), P("blk", "path"), P("blk")),
        check_vma=False,
    )
```
